128 devices in a mesh: dp: 4 (over x), block: 32 (over z, y, core).
Axes of the slice: x: 4, y: 4, z: 4, core: 2. Of those that a mesh axis runs over, the one named last changes fastest.
Arguments:
- tokens: bfloat16 [16384, 8192], P('dp', 'block'), may hold values from -6 to 6
- cotangent: bfloat16 [16384, 8192], P('dp', 'block'), may hold values from -0.09375 to 0.09375
- first_mean: float32 [64, 128, 128], P('block', 'dp'), may hold values from -0.5 to 0.5
- first_rho: float32 [64, 128, 128], P('block', 'dp'), may hold values from -4 to -2
- first_noise: float32 [64, 128, 128], P('block', 'dp'), may hold values from -6 to 6
- second_mean: float32 [128, 64, 512], P('block', 'dp'), may hold values from -0.75 to 0.75
- second_rho: float32 [128, 64, 512], P('block', 'dp'), may hold values from -4 to -2
- second_noise: float32 [128, 64, 512], P('block', 'dp'), may hold values from -6 to 6
- third_mean: float32 [128, 256, 64], P('block', 'dp'), may hold values from -0.375 to 0.375
- third_rho: float32 [128, 256, 64], P('block', 'dp'), may hold values from -4 to -2
- third_noise: float32 [128, 256, 64], P('block', 'dp'), may hold values from -6 to 6
- fourth_mean: float32 [64, 128, 128], P('block', 'dp'), may hold values from -0.5 to 0.5
- fourth_rho: float32 [64, 128, 128], P('block', 'dp'), may hold values from -4 to -2
- fourth_noise: float32 [64, 128, 128], P('block', 'dp'), may hold values from -6 to 6
Outputs:
- layer_out: bfloat16 [16384, 8192], P('dp', 'block')
- first_mean_grad: float32 [64, 128, 128], P('block', 'dp')
- first_rho_grad: float32 [64, 128, 128], P('block', 'dp')
- second_mean_grad: float32 [128, 64, 512], P('block', 'dp')
- second_rho_grad: float32 [128, 64, 512], P('block', 'dp')
- third_mean_grad: float32 [128, 256, 64], P('block', 'dp')
- third_rho_grad: float32 [128, 256, 64], P('block', 'dp')
- fourth_mean_grad: float32 [64, 128, 128], P('block', 'dp')
- fourth_rho_grad: float32 [64, 128, 128], P('block', 'dp')
The draws below stay inside these ranges and needn't reach their ends.
All inputs are finite; a program needn't handle non-finite values.
Results may differ from the reference program's by a relative error of at most 0.01.
Values may be sent and summed in bfloat16 or wider, within the bound.
No kernel may reach another device: no remote copies, remote signals or barrier semaphores. Data moves between devices by JAX's collectives and lax.ppermute only.
A program may use at most 192 MiB of HBM per device.

```python
import math
import jax
import jax.numpy as jnp
from jax import lax

D = 8192
BWIDTH = 128
TOK_DEV = 4096
NFIRST = 64
HBLK = 256
TOKENS = 16384


def block_levels(key, extent, shards, smallest, largest):
    def one(dim, blocks):
        draws = jax.random.uniform(jax.random.fold_in(jax.random.fold_in(key, 6), dim), (blocks,), jnp.float32, smallest / len(shards), largest / len(shards))
        return jnp.repeat(jnp.exp(draws), extent[dim] // blocks).reshape((-1,) + (1,) * (len(extent) - dim - 1))

    factor_of = one(*shards[0])
    for cut in shards[1:]:
        factor_of = factor_of * one(*cut)
    return factor_of


def normal_values(rng, dims, spread, limit, cuts=(), held_as=jnp.bfloat16):
    gain = block_levels(rng, dims, cuts, -0.22, 0.18) if cuts else 1.0
    result = jax.random.normal(rng, dims, jnp.float32) * spread * gain
    return jnp.minimum(jnp.maximum(result, -limit), limit).astype(held_as)


def setup_inputs(seed: int = 0) -> dict:
    splits = jax.random.split(jax.random.key(seed), 15)
    return {
        "tokens": normal_values(splits[0], (TOKENS, D), 1.0, 6.0, ((0, 4), (1, 32))),
        "cotangent": normal_values(splits[1], (TOKENS, D), (2 * TOKENS ** -0.5), 0.09375, ((0, 4), (1, 32))),
        "first_mean": normal_values(splits[2], (NFIRST, BWIDTH, BWIDTH), BWIDTH ** -0.5, 0.5, ((0, 32), (1, 4)), jnp.float32),
        "first_rho": jnp.clip(-4.0 + 2.0 * jax.random.uniform(splits[3], (NFIRST, BWIDTH, BWIDTH), jnp.float32) ** block_levels(splits[3], (NFIRST, BWIDTH, BWIDTH), ((0, 32), (1, 4)), -0.2, 0.2), -4.0, -2.0),
        "first_noise": normal_values(splits[4], (NFIRST, BWIDTH, BWIDTH), 1.0, 6.0, ((0, 32), (1, 4)), jnp.float32),
        "second_mean": normal_values(splits[5], (BWIDTH, NFIRST, 2 * HBLK), NFIRST ** -0.5, 0.75, ((0, 32), (1, 4)), jnp.float32),
        "second_rho": jnp.clip(-4.0 + 2.0 * jax.random.uniform(splits[6], (BWIDTH, NFIRST, 2 * HBLK), jnp.float32) ** block_levels(splits[6], (BWIDTH, NFIRST, 2 * HBLK), ((0, 32), (1, 4)), -0.2, 0.2), -4.0, -2.0),
        "second_noise": normal_values(splits[7], (BWIDTH, NFIRST, 2 * HBLK), 1.0, 6.0, ((0, 32), (1, 4)), jnp.float32),
        "third_mean": normal_values(splits[8], (BWIDTH, HBLK, NFIRST), HBLK ** -0.5, 0.375, ((0, 32), (1, 4)), jnp.float32),
        "third_rho": jnp.clip(-4.0 + 2.0 * jax.random.uniform(splits[9], (BWIDTH, HBLK, NFIRST), jnp.float32) ** block_levels(splits[9], (BWIDTH, HBLK, NFIRST), ((0, 32), (1, 4)), -0.2, 0.2), -4.0, -2.0),
        "third_noise": normal_values(splits[10], (BWIDTH, HBLK, NFIRST), 1.0, 6.0, ((0, 32), (1, 4)), jnp.float32),
        "fourth_mean": normal_values(splits[11], (NFIRST, BWIDTH, BWIDTH), BWIDTH ** -0.5, 0.5, ((0, 32), (1, 4)), jnp.float32),
        "fourth_rho": jnp.clip(-4.0 + 2.0 * jax.random.uniform(splits[12], (NFIRST, BWIDTH, BWIDTH), jnp.float32) ** block_levels(splits[12], (NFIRST, BWIDTH, BWIDTH), ((0, 32), (1, 4)), -0.2, 0.2), -4.0, -2.0),
        "fourth_noise": normal_values(splits[13], (NFIRST, BWIDTH, BWIDTH), 1.0, 6.0, ((0, 32), (1, 4)), jnp.float32),
    }


def rounded(value):
    return lax.optimization_barrier(value.astype(jnp.bfloat16)).astype(jnp.float32)


def sampled(mean, rho, noise):
    return rounded(mean + jax.nn.softplus(rho) * noise)


def reference(tokens, cotangent, first_mean, first_rho, first_noise, second_mean, second_rho, second_noise, third_mean, third_rho, third_noise, fourth_mean, fourth_rho, fourth_noise):
    weight_one = sampled(first_mean, first_rho, first_noise)
    weight_two = sampled(second_mean, second_rho, second_noise)
    weight_three = sampled(third_mean, third_rho, third_noise)
    weight_four = sampled(fourth_mean, fourth_rho, fourth_noise)
    rows = math.gcd(TOK_DEV, 512)
    blocks = TOKENS // rows
    token_blocks = tokens.reshape(blocks, rows, D)
    grad_blocks = cotangent.reshape(blocks, rows, D)

    def advance(carry, pair):
        acc_one, acc_two, acc_three, acc_four = carry
        token_rows, grad_rows = pair
        inputs = token_rows.reshape(rows, NFIRST, BWIDTH).astype(jnp.float32)
        first_out = rounded(jnp.einsum("tma,mac->tmc", inputs, weight_one))
        permuted = jnp.transpose(first_out, (0, 2, 1))
        gate_up = jnp.einsum("tcm,cme->tce", permuted, weight_two)
        gate = gate_up[..., :HBLK]
        upward = gate_up[..., HBLK:]
        hidden = rounded(jax.nn.silu(gate) * upward)
        third_out = rounded(jnp.einsum("tck,ckm->tcm", hidden, weight_three))
        returned = jnp.transpose(third_out, (0, 2, 1))
        output_rows = jnp.einsum("tmc,mcd->tmd", returned, weight_four).astype(jnp.bfloat16).reshape(rows, D)
        upstream = grad_rows.reshape(rows, NFIRST, BWIDTH).astype(jnp.float32)
        back_four = rounded(jnp.einsum("tmd,mcd->tmc", upstream, weight_four))
        term_four = jnp.einsum("tmc,tmd->mcd", returned, upstream)
        back_three = jnp.transpose(back_four, (0, 2, 1))
        hidden_grad = jnp.einsum("tcm,ckm->tck", back_three, weight_three)
        term_three = jnp.einsum("tck,tcm->ckm", hidden, back_three)
        sigma_gate = jax.nn.sigmoid(gate)
        gate_grad = hidden_grad * upward * sigma_gate * (1.0 + gate * (1.0 - sigma_gate))
        up_grad = hidden_grad * jax.nn.silu(gate)
        pair_grad = rounded(jnp.concatenate([gate_grad, up_grad], axis=-1))
        back_two = rounded(jnp.einsum("tce,cme->tcm", pair_grad, weight_two))
        term_two = jnp.einsum("tcm,tce->cme", permuted, pair_grad)
        back_one = jnp.transpose(back_two, (0, 2, 1))
        term_one = jnp.einsum("tma,tmc->mac", inputs, back_one)
        carry = (acc_one + term_one, acc_two + term_two, acc_three + term_three, acc_four + term_four)
        return carry, output_rows

    start = (jnp.zeros((NFIRST, BWIDTH, BWIDTH), jnp.float32), jnp.zeros((BWIDTH, NFIRST, 2 * HBLK), jnp.float32), jnp.zeros((BWIDTH, HBLK, NFIRST), jnp.float32), jnp.zeros((NFIRST, BWIDTH, BWIDTH), jnp.float32))
    totals, outputs = lax.scan(advance, start, (token_blocks, grad_blocks))
    total_one, total_two, total_three, total_four = totals
    layer_out = outputs.reshape(TOKENS, D)
    return (layer_out,
            total_one, total_one * first_noise * jax.nn.sigmoid(first_rho),
            total_two, total_two * second_noise * jax.nn.sigmoid(second_rho),
            total_three, total_three * third_noise * jax.nn.sigmoid(third_rho),
            total_four, total_four * fourth_noise * jax.nn.sigmoid(fourth_rho))
```

```python
import functools

import jax
import jax.numpy as jnp
from jax import lax
from jax.experimental import pallas as pl
from jax.experimental.pallas import tpu as pltpu
from jax.sharding import PartitionSpec as P

F32, BF16 = jnp.float32, jnp.bfloat16
EXACT = lax.Precision.HIGHEST
VMEM = pl.BlockSpec(memory_space=pltpu.VMEM)


def dot(a, b, ca, cb, **kw):
    return lax.dot_general(a, b, (((ca,), (cb,)), ((), ())), preferred_element_type=F32, **kw)


def sampled(mean, rho, noise):
    return (mean + jax.nn.softplus(rho) * noise).astype(BF16)


def params():
    return pltpu.CompilerParams(vmem_limit_bytes=50 * 2**20, dimension_semantics=("arbitrary",))


def gather_parts(part, n):
    return [part] + [lax.ppermute(part, "dp", [(j, (j + k) % n) for j in range(n)]) for k in range(1, n)]


def scatter_parts(parts, n):
    return [parts[0]] + [
        lax.ppermute(parts[k], "dp", [(j, (j + k) % n) for j in range(n)]) for k in range(1, n)
    ]


def exchange(x):
    return lax.all_to_all(x, "block", split_axis=0, concat_axis=0, tiled=True)


def place_m(m, owned_m, owned_c, rows, width, dtype):
    r = lax.broadcasted_iota(jnp.int32, (rows, width), 0)
    c = lax.broadcasted_iota(jnp.int32, (rows, width), 1)
    hit = (r // owned_c % owned_m == m) & (r // (owned_m * owned_c) * owned_c + r % owned_c == c)
    return jnp.where(hit, 1.0, 0.0).astype(dtype)


def place_c(c, owned_c, rows, width, dtype):
    r = lax.broadcasted_iota(jnp.int32, (rows, width), 0)
    m = lax.broadcasted_iota(jnp.int32, (rows, width), 1)
    return jnp.where((r % owned_c == c) & (r // owned_c == m), 1.0, 0.0).astype(dtype)


def owner(k, n):
    return lax.rem(lax.axis_index("dp") + (n + k), n)


def assemble(parts, full, n, first=0):
    size = parts[0].shape[1]
    for k in range(n):
        at = pl.multiple_of(owner(-k, n) * size, size)
        for i in range(full.shape[0]):
            full[i, pl.ds(at, size), :] = parts[k][first + i]


def split(full, outs, n):
    size = outs[0].shape[1]
    for k in range(n):
        at = pl.multiple_of(owner(k, n) * size, size)
        for i in range(full.shape[0]):
            outs[k][i] = full[i, pl.ds(at, size), :]


def outer_in_kernel(n, owned_c, contract, first, *refs):
    parts, (x, y, placed, full) = refs[:n], refs[n:]
    owned_m, width = full.shape[0], full.shape[2]

    @pl.when(pl.program_id(0) == 0)
    def _():
        assemble(parts, full, n, first)
        for m in range(owned_m):
            hot = place_m(m, owned_m, owned_c, placed.shape[0], width, BF16)
            placed[:, m * width : (m + 1) * width] = dot(hot, full[m], 1, contract).astype(BF16)

    y[...] = dot(placed[...], x[...], 1, 1).astype(BF16)


def outer_in(parts, x, n, owned_c, contract, first, tb):
    tokens, rows = x.shape
    owned_m = parts[0].shape[0] // 2
    width = parts[0].shape[2]
    return pl.pallas_call(
        functools.partial(outer_in_kernel, n, owned_c, contract, first),
        grid=(tokens // tb,),
        in_specs=[VMEM] * n + [pl.BlockSpec((tb, rows), lambda i: (i, 0))],
        out_specs=[pl.BlockSpec((rows, tb), lambda i: (0, i)), pl.BlockSpec((rows, rows), lambda i: (0, 0))],
        out_shape=[jax.ShapeDtypeStruct((rows, tokens), BF16), jax.ShapeDtypeStruct((rows, rows), BF16)],
        scratch_shapes=[pltpu.VMEM((owned_m, width, width), BF16)],
        compiler_params=params(),
        cost_estimate=pl.CostEstimate(flops=2 * tokens * rows * rows, bytes_accessed=4 * tokens * rows, transcendentals=0),
    )(*parts, x)


def outer_out_kernel(n, owned_m, owned_c, *refs):
    v, e, placed, out, *parts = refs[: 4 + n]
    total, full = refs[4 + n :]
    step, width = pl.program_id(0), full.shape[2]

    @pl.when(step == 0)
    def _():
        total[...] = jnp.zeros_like(total)

    out[...] = dot(v[...], placed[...], 0, 0).astype(BF16)
    total[...] += dot(v[...], e[...], 1, 0)

    @pl.when(step == pl.num_programs(0) - 1)
    def _():
        for m in range(owned_m):
            hot = place_m(m, owned_m, owned_c, total.shape[0], width, F32)
            full[m] = dot(hot, total[:, m * width : (m + 1) * width], 0, 0, precision=EXACT)
        split(full, parts, n)


def outer_out(v, e, placed, n, owned_m, owned_c, width, tb):
    tokens, rows = e.shape
    part = jax.ShapeDtypeStruct((owned_m, width // n, width), F32)
    return pl.pallas_call(
        functools.partial(outer_out_kernel, n, owned_m, owned_c),
        grid=(tokens // tb,),
        in_specs=[
            pl.BlockSpec((rows, tb), lambda i: (0, i)),
            pl.BlockSpec((tb, rows), lambda i: (i, 0)),
            pl.BlockSpec((rows, rows), lambda i: (0, 0)),
        ],
        out_specs=[pl.BlockSpec((tb, rows), lambda i: (i, 0))] + [pl.BlockSpec(part.shape, lambda i: (0, 0, 0))] * n,
        out_shape=[jax.ShapeDtypeStruct((tokens, rows), BF16)] + [part] * n,
        scratch_shapes=[pltpu.VMEM((rows, rows), F32), pltpu.VMEM((owned_m, width, width), F32)],
        compiler_params=params(),
        cost_estimate=pl.CostEstimate(flops=4 * tokens * rows * rows, bytes_accessed=6 * tokens * rows, transcendentals=0),
    )(v, e, placed)


def outer_grad_kernel(n, owned_m, owned_c, *refs):
    z, x, *parts = refs[: 2 + n]
    total, full = refs[2 + n :]
    step, width = pl.program_id(0), full.shape[2]

    @pl.when(step == 0)
    def _():
        total[...] = jnp.zeros_like(total)

    total[...] += dot(z[...], x[...], 1, 0)

    @pl.when(step == pl.num_programs(0) - 1)
    def _():
        for m in range(owned_m):
            hot = place_m(m, owned_m, owned_c, total.shape[0], width, F32)
            full[m] = dot(total[:, m * width : (m + 1) * width], hot, 0, 0, precision=EXACT)
        split(full, parts, n)


def outer_grad(z, x, n, owned_m, owned_c, width, tb):
    tokens, rows = x.shape
    part = jax.ShapeDtypeStruct((owned_m, width // n, width), F32)
    return pl.pallas_call(
        functools.partial(outer_grad_kernel, n, owned_m, owned_c),
        grid=(tokens // tb,),
        in_specs=[pl.BlockSpec((rows, tb), lambda i: (0, i)), pl.BlockSpec((tb, rows), lambda i: (i, 0))],
        out_specs=[pl.BlockSpec(part.shape, lambda i: (0, 0, 0))] * n,
        out_shape=[part] * n,
        scratch_shapes=[pltpu.VMEM((rows, rows), F32), pltpu.VMEM((owned_m, width, width), F32)],
        compiler_params=params(),
        cost_estimate=pl.CostEstimate(flops=2 * tokens * rows * rows, bytes_accessed=4 * tokens * rows, transcendentals=0),
    )(z, x)


def inner_fwd_kernel(n, *refs):
    parts2, parts3, (y, v, up2, down3) = refs[:n], refs[n : 2 * n], refs[2 * n : 2 * n + 4]
    full2, full3 = refs[2 * n + 4 :]
    owned_c, nm, pair = full2.shape
    half, rows = pair // 2, y.shape[0]

    @pl.when(pl.program_id(0) == 0)
    def _():
        assemble(parts2, full2, n)
        assemble(parts3, full3, n)
        for c in range(owned_c):
            hot = place_c(c, owned_c, rows, nm, BF16)
            up2[c * pair : (c + 1) * pair, :] = dot(full2[c], hot, 0, 1).astype(BF16)
            down3[:, c * half : (c + 1) * half] = dot(hot, full3[c], 1, 1).astype(BF16)

    block = y[...]
    total = None
    for c in range(owned_c):
        g = dot(up2[c * pair : (c + 1) * pair, :], block, 1, 0)
        gate, up = g[:half], g[half:]
        hidden = (gate * jax.nn.sigmoid(gate) * up).astype(BF16)
        term = dot(down3[:, c * half : (c + 1) * half], hidden, 1, 0)
        total = term if total is None else total + term
    v[...] = total.astype(BF16)


def inner_fwd(parts2, parts3, y, n, tb):
    rows, tokens = y.shape
    owned_c, nm, pair = parts2[0].shape[0], parts2[0].shape[1] * n, parts2[0].shape[2]
    half = pair // 2
    fixed = lambda i: (0, 0)
    return pl.pallas_call(
        functools.partial(inner_fwd_kernel, n),
        grid=(tokens // tb,),
        in_specs=[VMEM] * (2 * n) + [pl.BlockSpec((rows, tb), lambda i: (0, i))],
        out_specs=[
            pl.BlockSpec((rows, tb), lambda i: (0, i)),
            pl.BlockSpec((owned_c * pair, rows), fixed),
            pl.BlockSpec((rows, owned_c * half), fixed),
        ],
        out_shape=[
            jax.ShapeDtypeStruct((rows, tokens), BF16),
            jax.ShapeDtypeStruct((owned_c * pair, rows), BF16),
            jax.ShapeDtypeStruct((rows, owned_c * half), BF16),
        ],
        scratch_shapes=[pltpu.VMEM((owned_c, nm, pair), BF16), pltpu.VMEM((owned_c, half, nm), BF16)],
        compiler_params=params(),
        cost_estimate=pl.CostEstimate(
            flops=6 * tokens * rows * owned_c * half, bytes_accessed=4 * tokens * rows, transcendentals=tokens * owned_c * half
        ),
    )(*parts2, *parts3, y)


def inner_bwd_kernel(n, y, dv, up2, down3, dz, *refs):
    parts2, parts3 = refs[:n], refs[n : 2 * n]
    up3, down2, total2, total3, full2, full3 = refs[2 * n :]
    owned_c, nm, pair = full2.shape
    half, rows = pair // 2, y.shape[0]
    step = pl.program_id(0)

    @pl.when(step == 0)
    def _():
        total2[...] = jnp.zeros_like(total2)
        total3[...] = jnp.zeros_like(total3)
        up3[...] = down3[...].T
        down2[...] = up2[...].T

    block, back = y[...], dv[...]
    total = None
    for c in range(owned_c):
        pairs, halves = slice(c * pair, (c + 1) * pair), slice(c * half, (c + 1) * half)
        g = dot(up2[pairs, :], block, 1, 0)
        gate, up = g[:half], g[half:]
        sigma = jax.nn.sigmoid(gate)
        silu = gate * sigma
        hidden = (silu * up).astype(BF16)
        total3[halves, :] += dot(hidden, back, 1, 1)
        dh = dot(up3[halves, :], back, 1, 0)
        d_gate = (dh * up * (sigma + silu * (1.0 - sigma))).astype(BF16)
        d_up = (dh * silu).astype(BF16)
        dg = jnp.concatenate([d_gate, d_up], axis=0)
        total2[:, pairs] += dot(block, dg, 1, 1)
        term = dot(down2[:, pairs], dg, 1, 0)
        total = term if total is None else total + term
    dz[...] = total.astype(BF16)

    @pl.when(step == pl.num_programs(0) - 1)
    def _():
        for c in range(owned_c):
            hot = place_c(c, owned_c, rows, nm, F32)
            full2[c] = dot(hot, total2[:, c * pair : (c + 1) * pair], 0, 0, precision=EXACT)
            full3[c] = dot(total3[c * half : (c + 1) * half, :], hot, 1, 0, precision=EXACT)
        split(full2, parts2, n)
        split(full3, parts3, n)


def inner_bwd(y, dv, up2, down3, n, nm, owned_c, tb):
    rows, tokens = y.shape
    pair, half = up2.shape[0] // owned_c, down3.shape[1] // owned_c
    part2 = jax.ShapeDtypeStruct((owned_c, nm // n, pair), F32)
    part3 = jax.ShapeDtypeStruct((owned_c, half // n, nm), F32)
    fixed = lambda i: (0, 0)
    fixed3 = lambda i: (0, 0, 0)
    return pl.pallas_call(
        functools.partial(inner_bwd_kernel, n),
        grid=(tokens // tb,),
        in_specs=[
            pl.BlockSpec((rows, tb), lambda i: (0, i)),
            pl.BlockSpec((rows, tb), lambda i: (0, i)),
            pl.BlockSpec(up2.shape, fixed),
            pl.BlockSpec(down3.shape, fixed),
        ],
        out_specs=[pl.BlockSpec((rows, tb), lambda i: (0, i))]
        + [pl.BlockSpec(part2.shape, fixed3)] * n
        + [pl.BlockSpec(part3.shape, fixed3)] * n,
        out_shape=[jax.ShapeDtypeStruct((rows, tokens), BF16)] + [part2] * n + [part3] * n,
        scratch_shapes=[
            pltpu.VMEM((owned_c * half, rows), BF16),
            pltpu.VMEM((rows, owned_c * pair), BF16),
            pltpu.VMEM((rows, owned_c * pair), F32),
            pltpu.VMEM((owned_c * half, rows), F32),
            pltpu.VMEM((owned_c, nm, pair), F32),
            pltpu.VMEM((owned_c, half, nm), F32),
        ],
        compiler_params=params(),
        cost_estimate=pl.CostEstimate(
            flops=16 * tokens * rows * owned_c * half, bytes_accessed=6 * tokens * rows, transcendentals=tokens * owned_c * half
        ),
    )(y, dv, up2, down3)


def finish_kernel(n, *refs):
    parts, (rho, noise, mean_grad, rho_grad) = refs[:n], refs[n:]
    total = parts[0][...]
    for part in parts[1:]:
        total = total + part[...]
    mean_grad[...] = total
    rho_grad[...] = total * noise[...] * jax.nn.sigmoid(rho[...])


def finish(parts, rho, noise):
    n = len(parts)
    return pl.pallas_call(
        functools.partial(finish_kernel, n),
        in_specs=[VMEM] * (n + 2),
        out_specs=[VMEM] * 2,
        out_shape=[jax.ShapeDtypeStruct(rho.shape, F32)] * 2,
        compiler_params=pltpu.CompilerParams(vmem_limit_bytes=50 * 2**20),
    )(*parts, rho, noise)


def shards(
    n,
    tokens,
    cotangent,
    first_mean,
    first_rho,
    first_noise,
    second_mean,
    second_rho,
    second_noise,
    third_mean,
    third_rho,
    third_noise,
    fourth_mean,
    fourth_rho,
    fourth_noise,
):
    owned_m, width = first_mean.shape[0], first_mean.shape[2]
    owned_c, nm = second_mean.shape[0], second_mean.shape[1] * n
    tb = 512

    outer = jnp.concatenate(
        [sampled(first_mean, first_rho, first_noise), sampled(fourth_mean, fourth_rho, fourth_noise)], axis=0
    )
    outer_parts = gather_parts(outer, n)
    y_out, _ = outer_in(outer_parts, tokens, n, owned_c, 1, 0, 1024)
    y = exchange(y_out)
    back_out, placed4 = outer_in(outer_parts, cotangent, n, owned_c, 0, owned_m, 1024)
    back = exchange(back_out)
    parts2 = gather_parts(sampled(second_mean, second_rho, second_noise), n)
    parts3 = gather_parts(sampled(third_mean, third_rho, third_noise), n)
    v_out, up2, down3 = inner_fwd(parts2, parts3, y, n, tb)
    v = exchange(v_out)
    dz_out, *shares = inner_bwd(y, back, up2, down3, n, nm, owned_c, tb)
    dz = exchange(dz_out)
    two = finish(scatter_parts(shares[:n], n), second_rho, second_noise)
    three = finish(scatter_parts(shares[n:], n), third_rho, third_noise)
    layer_out, *share4 = outer_out(v, cotangent, placed4, n, owned_m, owned_c, width, 1024)
    four = finish(scatter_parts(share4, n), fourth_rho, fourth_noise)
    share1 = outer_grad(dz, tokens, n, owned_m, owned_c, width, 1024)
    one = finish(scatter_parts(share1, n), first_rho, first_noise)
    return (layer_out, *one, *two, *three, *four)


def solution(mesh):
    block = P("block", "dp", None)
    rows = P("dp", "block")
    return jax.shard_map(
        functools.partial(shards, mesh.shape["dp"]),
        mesh=mesh,
        in_specs=(rows, rows) + (block,) * 12,
        out_specs=(rows,) + (block,) * 8,
        check_vma=False,
    )
```

```python
import functools

import jax
import jax.numpy as jnp
from jax import lax
from jax.experimental import pallas as pl
from jax.experimental.pallas import tpu as pltpu
from jax.sharding import PartitionSpec as P

F32, BF16 = jnp.float32, jnp.bfloat16
VMEM = pl.BlockSpec(memory_space=pltpu.VMEM)
HBM = pl.BlockSpec(memory_space=pltpu.HBM)
LANES = 128


def dot(a, b, ca, cb, **kw):
    return lax.dot_general(a, b, (((ca,), (cb,)), ((), ())), preferred_element_type=F32, **kw)


def picked(a, b, ca, cb):
    total = None
    first = a.dtype == BF16
    rest = b if first else a
    for _ in range(3):
        part = rest.astype(BF16)
        rest = rest - part.astype(F32)
        term = dot(a, part, ca, cb) if first else dot(part, b, ca, cb)
        total = term if total is None else total + term
    return total


def logistic(v):
    return 0.5 * jnp.tanh(0.5 * v) + 0.5


def sampled(mean, rho, noise):
    return (mean + jax.nn.softplus(rho) * noise).astype(BF16)


def params(mib):
    return pltpu.CompilerParams(vmem_limit_bytes=mib * 2**20, dimension_semantics=("arbitrary",))


def gather_parts(part, n):
    return [part] + [lax.ppermute(part, "dp", [(j, (j + k) % n) for j in range(n)]) for k in range(1, n)]


def scatter_parts(parts, n):
    return [parts[0]] + [
        lax.ppermute(parts[k], "dp", [(j, (j + k) % n) for j in range(n)]) for k in range(1, n)
    ]


def exchange(x):
    return lax.all_to_all(x, "block", split_axis=0, concat_axis=0, tiled=True)


def place_m(m, owned_m, owned_c, rows, width, dtype):
    r = lax.broadcasted_iota(jnp.int32, (rows, width), 0)
    c = lax.broadcasted_iota(jnp.int32, (rows, width), 1)
    hit = (r // owned_c % owned_m == m) & (r // (owned_m * owned_c) * owned_c + r % owned_c == c)
    return jnp.where(hit, 1.0, 0.0).astype(dtype)


def place_c(c, owned_c, rows, width, dtype):
    r = lax.broadcasted_iota(jnp.int32, (rows, width), 0)
    m = lax.broadcasted_iota(jnp.int32, (rows, width), 1)
    return jnp.where((r % owned_c == c) & (r // owned_c == m), 1.0, 0.0).astype(dtype)


def owner(k, n):
    return lax.rem(lax.axis_index("dp") + (n + k), n)


def assemble(parts, full, n, first=0):
    size = parts[0].shape[1]
    for k in range(n):
        at = pl.multiple_of(owner(-k, n) * size, size)
        for i in range(full.shape[0]):
            full[i, pl.ds(at, size), :] = parts[k][first + i]


def split(full, outs, n):
    size = outs[0].shape[1]
    for k in range(n):
        at = pl.multiple_of(owner(k, n) * size, size)
        for i in range(full.shape[0]):
            outs[k][i] = full[i, pl.ds(at, size), :]


def chunks(total, count):
    size = total // count
    return [slice(k * size, (k + 1) * size) for k in range(count)]


def stash_kernel(count, x, *refs):
    held, done = refs[-2:]
    copies = [
        pltpu.make_async_copy(x.at[rows], held.at[rows], done.at[k]) for k, rows in enumerate(chunks(x.shape[0], count))
    ]
    for copy in copies:
        copy.start()
    for copy in copies:
        copy.wait()


def stash(x, after=()):
    count = 4
    return pl.pallas_call(
        functools.partial(stash_kernel, count),
        in_specs=[HBM] * (1 + len(after)),
        out_specs=VMEM,
        out_shape=pltpu.VMEM(x.shape, x.dtype),
        scratch_shapes=[pltpu.SemaphoreType.DMA((count,))],
        compiler_params=pltpu.CompilerParams(vmem_limit_bytes=16 * 2**20),
        cost_estimate=pl.CostEstimate(flops=0, bytes_accessed=4 * x.size, transcendentals=0),
    )(x, *after)


def outer_in_kernel(n, owned_c, contract, first, count, *refs):
    parts, x = refs[:n], refs[n]
    y, placed, full, held, done = refs[-5:]
    owned_m, width = full.shape[0], full.shape[2]
    assemble(parts, full, n, first)
    for m in range(owned_m):
        hot = place_m(m, owned_m, owned_c, placed.shape[0], width, BF16)
        placed[:, m * width : (m + 1) * width] = dot(hot, full[m], 1, contract).astype(BF16)
    copies = []
    for k, cols in enumerate(chunks(x.shape[0], count)):
        held[:, cols] = dot(placed[...], x[cols, :], 1, 1).astype(BF16)
        copies.append(pltpu.make_async_copy(held.at[:, cols], y.at[:, cols], done.at[k]))
        copies[k].start()
    for copy in copies:
        copy.wait()


def outer_in(parts, x, n, owned_c, contract, first, after=()):
    tokens, rows = x.shape
    owned_m, width = parts[0].shape[0] // 2, parts[0].shape[2]
    count = 4
    return pl.pallas_call(
        functools.partial(outer_in_kernel, n, owned_c, contract, first, count),
        in_specs=[VMEM] * (n + 1) + [HBM] * len(after),
        out_specs=[HBM, VMEM],
        out_shape=[pltpu.HBM((rows, tokens), BF16), jax.ShapeDtypeStruct((rows, rows), BF16)],
        scratch_shapes=[
            pltpu.VMEM((owned_m, width, width), BF16),
            pltpu.VMEM((rows, tokens), BF16),
            pltpu.SemaphoreType.DMA((count,)),
        ],
        compiler_params=pltpu.CompilerParams(vmem_limit_bytes=24 * 2**20),
        cost_estimate=pl.CostEstimate(flops=2 * tokens * rows * rows, bytes_accessed=4 * tokens * rows, transcendentals=0),
    )(*parts, x, *after)


def outer_out_kernel(n, owned_m, owned_c, *refs):
    v, e, placed, out, *parts = refs[: 4 + n]
    total, full = refs[4 + n :]
    step, width = pl.program_id(0), full.shape[2]

    @pl.when(step == 0)
    def _():
        total[...] = jnp.zeros_like(total)

    out[...] = dot(v[...], placed[...], 0, 0).astype(BF16)
    total[...] += dot(v[...], e[...], 1, 0)

    @pl.when(step == pl.num_programs(0) - 1)
    def _():
        for m in range(owned_m):
            hot = place_m(m, owned_m, owned_c, total.shape[0], width, BF16)
            full[m] = picked(hot, total[:, m * width : (m + 1) * width], 0, 0)
        split(full, parts, n)


def outer_out(v, e, placed, n, owned_m, owned_c, width, tb):
    tokens, rows = e.shape
    part = jax.ShapeDtypeStruct((owned_m, width // n, width), F32)
    return pl.pallas_call(
        functools.partial(outer_out_kernel, n, owned_m, owned_c),
        grid=(tokens // tb,),
        in_specs=[
            pl.BlockSpec((rows, tb), lambda i: (0, i)),
            pl.BlockSpec((tb, rows), lambda i: (i, 0)),
            pl.BlockSpec((rows, rows), lambda i: (0, 0)),
        ],
        out_specs=[pl.BlockSpec((tb, rows), lambda i: (i, 0))] + [pl.BlockSpec(part.shape, lambda i: (0, 0, 0))] * n,
        out_shape=[jax.ShapeDtypeStruct((tokens, rows), BF16)] + [part] * n,
        scratch_shapes=[pltpu.VMEM((rows, rows), F32), pltpu.VMEM((owned_m, width, width), F32)],
        compiler_params=params(24),
        cost_estimate=pl.CostEstimate(flops=4 * tokens * rows * rows, bytes_accessed=6 * tokens * rows, transcendentals=0),
    )(v, e, placed)


def outer_grad_kernel(n, owned_m, owned_c, count, *refs):
    z, x = refs[:2]
    *parts, held, full, done = refs[-n - 3 :]
    width = full.shape[2]
    pieces = chunks(x.shape[0], count)
    copies = [pltpu.make_async_copy(z.at[:, cols], held.at[:, cols], done.at[k]) for k, cols in enumerate(pieces)]
    for copy in copies:
        copy.start()
    total = None
    for copy, cols in zip(copies, pieces):
        copy.wait()
        term = dot(held[:, cols], x[cols, :], 1, 0)
        total = term if total is None else total + term
    for m in range(owned_m):
        hot = place_m(m, owned_m, owned_c, total.shape[0], width, BF16)
        full[m] = picked(total[:, m * width : (m + 1) * width], hot, 0, 0)
    split(full, parts, n)


def outer_grad(z, x, n, owned_m, owned_c, width):
    tokens, rows = x.shape
    count = 4
    part = jax.ShapeDtypeStruct((owned_m, width // n, width), F32)
    return pl.pallas_call(
        functools.partial(outer_grad_kernel, n, owned_m, owned_c, count),
        in_specs=[HBM, VMEM],
        out_specs=[VMEM] * n,
        out_shape=[part] * n,
        scratch_shapes=[
            pltpu.VMEM((rows, tokens), BF16),
            pltpu.VMEM((owned_m, width, width), F32),
            pltpu.SemaphoreType.DMA((count,)),
        ],
        compiler_params=pltpu.CompilerParams(vmem_limit_bytes=24 * 2**20),
        cost_estimate=pl.CostEstimate(flops=2 * tokens * rows * rows, bytes_accessed=4 * tokens * rows, transcendentals=0),
    )(z, x)


def pack_shape(owned_c, own2, pair, own3, nm):
    assert own2 * (pair // LANES) == own3 and 2 * nm == LANES and owned_c % 2 == 0
    return (owned_c + owned_c // 2, own3, LANES)


def each_piece2(owned_c, own2, pair):
    for c in range(owned_c):
        for piece in range(pair // LANES):
            yield c, slice(piece * own2, (piece + 1) * own2), slice(piece * LANES, (piece + 1) * LANES)


def each_piece3(owned_c, nm):
    for c in range(owned_c):
        yield c, owned_c + c // 2, slice(c % 2 * nm, (c % 2 + 1) * nm)


def sample_kernel(mean2, rho2, noise2, mean3, rho3, noise3, *refs):
    packed = refs[-1]
    owned_c, own2, pair = mean2.shape
    for c, rows, cols in each_piece2(owned_c, own2, pair):
        packed[c, rows, :] = sampled(mean2[c, :, cols], rho2[c, :, cols], noise2[c, :, cols])
    for c, at, cols in each_piece3(owned_c, mean3.shape[2]):
        packed[at, :, cols] = sampled(mean3[c], rho3[c], noise3[c])


def sample_inner(second, third, after=()):
    shape = pack_shape(*second[0].shape, *third[0].shape[1:])
    return pl.pallas_call(
        sample_kernel,
        in_specs=[VMEM] * 6 + [HBM] * len(after),
        out_specs=VMEM,
        out_shape=jax.ShapeDtypeStruct(shape, BF16),
        compiler_params=pltpu.CompilerParams(vmem_limit_bytes=16 * 2**20),
    )(*second, *third, *after)


def inner_fwd_kernel(n, *refs):
    parts, (y, v, up2, down3) = refs[:n], refs[n : n + 4]
    full2, full3 = refs[n + 4 :]
    owned_c, nm, pair = full2.shape
    half, rows = pair // 2, y.shape[0]
    own2, own3 = nm // n, half // n

    @pl.when(pl.program_id(0) == 0)
    def _():
        for k in range(n):
            at2 = pl.multiple_of(owner(-k, n) * own2, own2)
            at3 = pl.multiple_of(owner(-k, n) * own3, own3)
            for c, piece, cols in each_piece2(owned_c, own2, pair):
                full2[c, pl.ds(at2, own2), cols] = parts[k][c, piece, :]
            for c, at, cols in each_piece3(owned_c, nm):
                full3[c, pl.ds(at3, own3), :] = parts[k][at, :, cols]
        for c in range(owned_c):
            hot = place_c(c, owned_c, rows, nm, BF16)
            up2[c * pair : (c + 1) * pair, :] = dot(full2[c], hot, 0, 1).astype(BF16)
            down3[:, c * half : (c + 1) * half] = dot(hot, full3[c], 1, 1).astype(BF16)

    block = y[...]
    total = None
    for c in range(owned_c):
        g = dot(up2[c * pair : (c + 1) * pair, :], block, 1, 0)
        gate, up = g[:half], g[half:]
        hidden = (gate * logistic(gate) * up).astype(BF16)
        term = dot(down3[:, c * half : (c + 1) * half], hidden, 1, 0)
        total = term if total is None else total + term
    v[...] = total.astype(BF16)


def inner_fwd(parts, y, n, owned_c, nm, half, tb):
    rows, tokens = y.shape
    pair = 2 * half
    fixed = lambda i: (0, 0)
    return pl.pallas_call(
        functools.partial(inner_fwd_kernel, n),
        grid=(tokens // tb,),
        in_specs=[VMEM] * n + [pl.BlockSpec((rows, tb), lambda i: (0, i))],
        out_specs=[
            pl.BlockSpec((rows, tb), lambda i: (0, i)),
            pl.BlockSpec((owned_c * pair, rows), fixed),
            pl.BlockSpec((rows, owned_c * half), fixed),
        ],
        out_shape=[
            pltpu.HBM((rows, tokens), BF16),
            pltpu.HBM((owned_c * pair, rows), BF16),
            pltpu.HBM((rows, owned_c * half), BF16),
        ],
        scratch_shapes=[pltpu.VMEM((owned_c, nm, pair), BF16), pltpu.VMEM((owned_c, half, nm), BF16)],
        compiler_params=params(32),
        cost_estimate=pl.CostEstimate(
            flops=6 * tokens * rows * owned_c * half, bytes_accessed=4 * tokens * rows, transcendentals=tokens * owned_c * half
        ),
    )(*parts, y)


def inner_bwd_kernel(n, owned_c, y, dv, up2, down3, dz, *refs):
    parts, (up3, down2, total2, total3) = refs[:n], refs[n:]
    rows = y.shape[0]
    nm, pair = rows // owned_c, up2.shape[0] // owned_c
    half = pair // 2
    own2, own3 = nm // n, half // n
    step = pl.program_id(0)

    @pl.when(step == 0)
    def _():
        total2[...] = jnp.zeros_like(total2)
        total3[...] = jnp.zeros_like(total3)
        up3[...] = down3[...].T
        down2[...] = up2[...].T

    block, back = y[...], dv[...]
    back_t = back.T
    total = None
    for c in range(owned_c):
        pairs, halves = slice(c * pair, (c + 1) * pair), slice(c * half, (c + 1) * half)
        g = dot(up2[pairs, :], block, 1, 0)
        gate, up = g[:half], g[half:]
        sigma = logistic(gate)
        silu = gate * sigma
        hidden = (silu * up).astype(BF16)
        total3[halves, :] += dot(hidden, back_t, 1, 0)
        dh = dot(up3[halves, :], back, 1, 0)
        d_gate = (dh * up * (sigma + silu * (1.0 - sigma))).astype(BF16)
        d_up = (dh * silu).astype(BF16)
        dg = jnp.concatenate([d_gate, d_up], axis=0)
        both = dot(block, dg, 1, 1)
        for piece in range(pair // LANES):
            total2[c * (pair // LANES) + piece] += both[:, piece * LANES : (piece + 1) * LANES]
        term = dot(down2[:, pairs], dg, 1, 0)
        total = term if total is None else total + term
    dz[...] = total.astype(BF16)

    @pl.when(step == pl.num_programs(0) - 1)
    def _():
        for k in range(n):
            at2 = owner(k, n) * (own2 * owned_c)
            for c, piece, cols in each_piece2(owned_c, own2, pair):
                held = total2.at[(c * pair + cols.start) // LANES]
                parts[k][c, piece, :] = held[pl.ds(at2 + c, own2, stride=owned_c), :]
        for c, at, cols in each_piece3(owned_c, nm):
            hot = place_c(c, owned_c, rows, nm, BF16)
            for k in range(n):
                at3 = pl.multiple_of(c * half + owner(k, n) * own3, own3)
                parts[k][at, :, cols] = picked(total3[pl.ds(at3, own3), :], hot, 1, 0)


def inner_bwd(y, dv, up2, down3, n, owned_c, tb):
    rows, tokens = y.shape
    pair, half, nm = up2.shape[0] // owned_c, down3.shape[1] // owned_c, rows // owned_c
    part = jax.ShapeDtypeStruct(pack_shape(owned_c, nm // n, pair, half // n, nm), F32)
    fixed = lambda i: (0, 0)
    fixed3 = lambda i: (0, 0, 0)
    return pl.pallas_call(
        functools.partial(inner_bwd_kernel, n, owned_c),
        grid=(tokens // tb,),
        in_specs=[
            pl.BlockSpec((rows, tb), lambda i: (0, i)),
            pl.BlockSpec((rows, tb), lambda i: (0, i)),
            pl.BlockSpec(up2.shape, fixed),
            pl.BlockSpec(down3.shape, fixed),
        ],
        out_specs=[pl.BlockSpec((rows, tb), lambda i: (0, i))] + [pl.BlockSpec(part.shape, fixed3)] * n,
        out_shape=[pltpu.HBM((rows, tokens), BF16)] + [pltpu.HBM(part.shape, part.dtype)] * n,
        scratch_shapes=[
            pltpu.VMEM((owned_c * half, rows), BF16),
            pltpu.VMEM((rows, owned_c * pair), BF16),
            pltpu.VMEM((owned_c * pair // LANES, rows, LANES), F32),
            pltpu.VMEM((owned_c * half, rows), F32),
        ],
        compiler_params=params(32),
        cost_estimate=pl.CostEstimate(
            flops=16 * tokens * rows * owned_c * half, bytes_accessed=6 * tokens * rows, transcendentals=tokens * owned_c * half
        ),
    )(y, dv, *(pltpu.with_memory_space_constraint(w, pltpu.HBM) for w in (up2, down3)))


def added(parts):
    total = parts[0]
    for part in parts[1:]:
        total = total + part
    return total


def finish_inner_kernel(n, *refs):
    parts, (rho2, noise2, rho3, noise3, mean2, grad2, mean3, grad3) = refs[:n], refs[n:]
    owned_c, own2, pair = rho2.shape
    for c, rows, cols in each_piece2(owned_c, own2, pair):
        total = added([part[c, rows, :] for part in parts])
        mean2[c, :, cols] = total
        grad2[c, :, cols] = total * noise2[c, :, cols] * logistic(rho2[c, :, cols])
    for c, at, cols in each_piece3(owned_c, rho3.shape[2]):
        total = added([part[at, :, cols] for part in parts])
        mean3[c] = total
        grad3[c] = total * noise3[c] * logistic(rho3[c])


def finish_inner(parts, rho2, noise2, rho3, noise3):
    n = len(parts)
    return pl.pallas_call(
        functools.partial(finish_inner_kernel, n),
        in_specs=[VMEM] * (n + 4),
        out_specs=[VMEM] * 4,
        out_shape=[jax.ShapeDtypeStruct(rho2.shape, F32)] * 2 + [jax.ShapeDtypeStruct(rho3.shape, F32)] * 2,
        compiler_params=pltpu.CompilerParams(vmem_limit_bytes=16 * 2**20),
    )(*parts, rho2, noise2, rho3, noise3)


def finish_kernel(n, *refs):
    parts, (rho, noise, mean_grad, rho_grad) = refs[:n], refs[n:]
    total = added([part[...] for part in parts])
    mean_grad[...] = total
    rho_grad[...] = total * noise[...] * logistic(rho[...])


def finish(parts, rho, noise):
    n = len(parts)
    return pl.pallas_call(
        functools.partial(finish_kernel, n),
        in_specs=[VMEM] * (n + 2),
        out_specs=[VMEM] * 2,
        out_shape=[jax.ShapeDtypeStruct(rho.shape, F32)] * 2,
        compiler_params=pltpu.CompilerParams(vmem_limit_bytes=16 * 2**20),
    )(*parts, rho, noise)


def shards(
    n,
    tokens,
    cotangent,
    first_mean,
    first_rho,
    first_noise,
    second_mean,
    second_rho,
    second_noise,
    third_mean,
    third_rho,
    third_noise,
    fourth_mean,
    fourth_rho,
    fourth_noise,
):
    owned_m, width = first_mean.shape[0], first_mean.shape[2]
    owned_c, nm = second_mean.shape[0], second_mean.shape[1] * n
    half = third_mean.shape[1] * n

    outer = jnp.concatenate(
        [sampled(first_mean, first_rho, first_noise), sampled(fourth_mean, fourth_rho, fourth_noise)], axis=0
    )
    outer_parts = gather_parts(outer, n)
    y_out, placed1 = outer_in(outer_parts, stash(tokens), n, owned_c, 1, 0)
    y = exchange(y_out)
    inner = sample_inner((second_mean, second_rho, second_noise), (third_mean, third_rho, third_noise), (placed1,))
    inner_parts = gather_parts(inner, n)
    back_out, placed4 = outer_in(outer_parts, cotangent, n, owned_c, 0, owned_m, inner_parts)
    back = exchange(back_out)
    v_out, up2, down3 = inner_fwd(inner_parts, y, n, owned_c, nm, half, 1024)
    v = exchange(v_out)
    dz_out, *shares = inner_bwd(y, back, up2, down3, n, owned_c, 1024)
    dz = exchange(dz_out)
    two_three = finish_inner(scatter_parts(shares, n), second_rho, second_noise, third_rho, third_noise)
    layer_out, *share4 = outer_out(v, cotangent, placed4, n, owned_m, owned_c, width, 2048)
    four = finish(scatter_parts(share4, n), fourth_rho, fourth_noise)
    share1 = outer_grad(dz, stash(tokens, (two_three[0], four[0])), n, owned_m, owned_c, width)
    one = finish(scatter_parts(share1, n), first_rho, first_noise)
    return (layer_out, *one, *two_three, *four)


def solution(mesh):
    block = P("block", "dp", None)
    rows = P("dp", "block")
    return jax.shard_map(
        functools.partial(shards, mesh.shape["dp"]),
        mesh=mesh,
        in_specs=(rows, rows) + (block,) * 12,
        out_specs=(rows,) + (block,) * 8,
        check_vma=False,
    )
```

```python
import functools

import jax
import jax.numpy as jnp
from jax import lax
from jax.experimental import pallas as pl
from jax.experimental.pallas import tpu as pltpu
from jax.sharding import PartitionSpec as P

F32, BF16 = jnp.float32, jnp.bfloat16
VMEM = pl.BlockSpec(memory_space=pltpu.VMEM)
HBM = pl.BlockSpec(memory_space=pltpu.HBM)
LANES = 128


def dot(a, b, ca, cb, **kw):
    return lax.dot_general(a, b, (((ca,), (cb,)), ((), ())), preferred_element_type=F32, **kw)


def picked(a, b, ca, cb):
    total = None
    first = a.dtype == BF16
    rest = b if first else a
    for _ in range(3):
        part = rest.astype(BF16)
        rest = rest - part.astype(F32)
        term = dot(a, part, ca, cb) if first else dot(part, b, ca, cb)
        total = term if total is None else total + term
    return total


def logistic(v):
    return 0.5 * jnp.tanh(0.5 * v) + 0.5


def sampled(mean, rho, noise):
    return (mean + jax.nn.softplus(rho) * noise).astype(BF16)


def params(mib):
    return pltpu.CompilerParams(vmem_limit_bytes=mib * 2**20, dimension_semantics=("arbitrary",))


def gather_parts(part, n):
    return [part] + [lax.ppermute(part, "dp", [(j, (j + k) % n) for j in range(n)]) for k in range(1, n)]


def scatter_parts(parts, n):
    return [parts[0]] + [
        lax.ppermute(parts[k], "dp", [(j, (j + k) % n) for j in range(n)]) for k in range(1, n)
    ]


def exchange(x):
    return lax.all_to_all(x, "block", split_axis=0, concat_axis=0, tiled=True)


def place_m(m, owned_m, owned_c, rows, width, dtype):
    r = lax.broadcasted_iota(jnp.int32, (rows, width), 0)
    c = lax.broadcasted_iota(jnp.int32, (rows, width), 1)
    hit = (r // owned_c % owned_m == m) & (r // (owned_m * owned_c) * owned_c + r % owned_c == c)
    return jnp.where(hit, 1.0, 0.0).astype(dtype)


def place_c(c, owned_c, rows, width, dtype):
    r = lax.broadcasted_iota(jnp.int32, (rows, width), 0)
    m = lax.broadcasted_iota(jnp.int32, (rows, width), 1)
    return jnp.where((r % owned_c == c) & (r // owned_c == m), 1.0, 0.0).astype(dtype)


def owner(k, n):
    return lax.rem(lax.axis_index("dp") + (n + k), n)


def assemble(parts, full, n, first=0):
    size = parts[0].shape[1]
    for k in range(n):
        at = pl.multiple_of(owner(-k, n) * size, size)
        for i in range(full.shape[0]):
            full[i, pl.ds(at, size), :] = parts[k][first + i]


def split(full, outs, n):
    size = outs[0].shape[1]
    for k in range(n):
        at = pl.multiple_of(owner(k, n) * size, size)
        for i in range(full.shape[0]):
            outs[k][i] = full[i, pl.ds(at, size), :]


def chunks(total, count):
    size = total // count
    return [slice(k * size, (k + 1) * size) for k in range(count)]


def stash_kernel(count, x, *refs):
    held, done = refs[-2:]
    copies = [
        pltpu.make_async_copy(x.at[rows], held.at[rows], done.at[k]) for k, rows in enumerate(chunks(x.shape[0], count))
    ]
    for copy in copies:
        copy.start()
    for copy in copies:
        copy.wait()


def stash(x, after=()):
    count = 4
    return pl.pallas_call(
        functools.partial(stash_kernel, count),
        in_specs=[HBM] * (1 + len(after)),
        out_specs=VMEM,
        out_shape=pltpu.VMEM(x.shape, x.dtype),
        scratch_shapes=[pltpu.SemaphoreType.DMA((count,))],
        compiler_params=pltpu.CompilerParams(vmem_limit_bytes=16 * 2**20),
        cost_estimate=pl.CostEstimate(flops=0, bytes_accessed=4 * x.size, transcendentals=0),
    )(x, *after)


def outer_in_kernel(n, owned_c, contract, first, count, *refs):
    parts, x = refs[:n], refs[n]
    y, placed, full, held, done = refs[-5:]
    owned_m, width = full.shape[0], full.shape[2]
    assemble(parts, full, n, first)
    for m in range(owned_m):
        hot = place_m(m, owned_m, owned_c, placed.shape[0], width, BF16)
        placed[:, m * width : (m + 1) * width] = dot(hot, full[m], 1, contract).astype(BF16)
    copies = []
    for k, cols in enumerate(chunks(x.shape[0], count)):
        held[:, cols] = dot(placed[...], x[cols, :], 1, 1).astype(BF16)
        copies.append(pltpu.make_async_copy(held.at[:, cols], y.at[:, cols], done.at[k]))
        copies[k].start()
    for copy in copies:
        copy.wait()


def outer_in(parts, x, n, owned_c, contract, first, after=()):
    tokens, rows = x.shape
    owned_m, width = parts[0].shape[0] // 2, parts[0].shape[2]
    count = 4
    return pl.pallas_call(
        functools.partial(outer_in_kernel, n, owned_c, contract, first, count),
        in_specs=[VMEM] * (n + 1) + [HBM] * len(after),
        out_specs=[HBM, VMEM],
        out_shape=[pltpu.HBM((rows, tokens), BF16), jax.ShapeDtypeStruct((rows, rows), BF16)],
        scratch_shapes=[
            pltpu.VMEM((owned_m, width, width), BF16),
            pltpu.VMEM((rows, tokens), BF16),
            pltpu.SemaphoreType.DMA((count,)),
        ],
        compiler_params=pltpu.CompilerParams(vmem_limit_bytes=24 * 2**20),
        cost_estimate=pl.CostEstimate(flops=2 * tokens * rows * rows, bytes_accessed=4 * tokens * rows, transcendentals=0),
    )(*parts, x, *after)


def outer_out_kernel(n, owned_m, owned_c, *refs):
    v, e, placed, out, *parts = refs[: 4 + n]
    total, full = refs[4 + n :]
    step, width = pl.program_id(0), full.shape[2]

    @pl.when(step == 0)
    def _():
        total[...] = jnp.zeros_like(total)

    out[...] = dot(v[...], placed[...], 0, 0).astype(BF16)
    total[...] += dot(v[...], e[...], 1, 0)

    @pl.when(step == pl.num_programs(0) - 1)
    def _():
        for m in range(owned_m):
            hot = place_m(m, owned_m, owned_c, total.shape[0], width, BF16)
            full[m] = picked(hot, total[:, m * width : (m + 1) * width], 0, 0)
        split(full, parts, n)


def outer_out(v, e, placed, n, owned_m, owned_c, width, tb):
    tokens, rows = e.shape
    part = jax.ShapeDtypeStruct((owned_m, width // n, width), F32)
    return pl.pallas_call(
        functools.partial(outer_out_kernel, n, owned_m, owned_c),
        grid=(tokens // tb,),
        in_specs=[
            pl.BlockSpec((rows, tb), lambda i: (0, i)),
            pl.BlockSpec((tb, rows), lambda i: (i, 0)),
            pl.BlockSpec((rows, rows), lambda i: (0, 0)),
        ],
        out_specs=[pl.BlockSpec((tb, rows), lambda i: (i, 0))] + [pl.BlockSpec(part.shape, lambda i: (0, 0, 0))] * n,
        out_shape=[jax.ShapeDtypeStruct((tokens, rows), BF16)] + [part] * n,
        scratch_shapes=[pltpu.VMEM((rows, rows), F32), pltpu.VMEM((owned_m, width, width), F32)],
        compiler_params=params(24),
        cost_estimate=pl.CostEstimate(flops=4 * tokens * rows * rows, bytes_accessed=6 * tokens * rows, transcendentals=0),
    )(v, e, placed)


def outer_grad_kernel(n, owned_m, owned_c, count, *refs):
    z, x = refs[:2]
    *parts, held, full, done = refs[-n - 3 :]
    width = full.shape[2]
    pieces = chunks(x.shape[0], count)
    copies = [pltpu.make_async_copy(z.at[at], held.at[at], done.at[k]) for k, at in enumerate(chunks(z.shape[0], count))]
    for copy in copies:
        copy.start()
    for copy in copies:
        copy.wait()
    total = dot(held[...], x[...], 1, 0)
    for m in range(owned_m):
        hot = place_m(m, owned_m, owned_c, total.shape[0], width, BF16)
        full[m] = picked(total[:, m * width : (m + 1) * width], hot, 0, 0)
    split(full, parts, n)


def outer_grad(z, x, n, owned_m, owned_c, width):
    tokens, rows = x.shape
    count = 4
    part = jax.ShapeDtypeStruct((owned_m, width // n, width), F32)
    return pl.pallas_call(
        functools.partial(outer_grad_kernel, n, owned_m, owned_c, count),
        in_specs=[HBM, VMEM],
        out_specs=[VMEM] * n,
        out_shape=[part] * n,
        scratch_shapes=[
            pltpu.VMEM((rows, tokens), BF16),
            pltpu.VMEM((owned_m, width, width), F32),
            pltpu.SemaphoreType.DMA((count,)),
        ],
        compiler_params=pltpu.CompilerParams(vmem_limit_bytes=24 * 2**20),
        cost_estimate=pl.CostEstimate(flops=2 * tokens * rows * rows, bytes_accessed=4 * tokens * rows, transcendentals=0),
    )(z, x)


def pack_shape(owned_c, own2, pair, own3, nm):
    assert own2 * (pair // LANES) == own3 and 2 * nm == LANES and owned_c % 2 == 0
    return (owned_c + owned_c // 2, own3, LANES)


def each_piece2(owned_c, own2, pair):
    for c in range(owned_c):
        for piece in range(pair // LANES):
            yield c, slice(piece * own2, (piece + 1) * own2), slice(piece * LANES, (piece + 1) * LANES)


def each_piece3(owned_c, nm):
    for c in range(owned_c):
        yield c, owned_c + c // 2, slice(c % 2 * nm, (c % 2 + 1) * nm)


def sample_kernel(mean2, rho2, noise2, mean3, rho3, noise3, *refs):
    packed = refs[-1]
    owned_c, own2, pair = mean2.shape
    for c, rows, cols in each_piece2(owned_c, own2, pair):
        packed[c, rows, :] = sampled(mean2[c, :, cols], rho2[c, :, cols], noise2[c, :, cols])
    for c, at, cols in each_piece3(owned_c, mean3.shape[2]):
        packed[at, :, cols] = sampled(mean3[c], rho3[c], noise3[c])


def sample_inner(second, third, after=()):
    shape = pack_shape(*second[0].shape, *third[0].shape[1:])
    return pl.pallas_call(
        sample_kernel,
        in_specs=[VMEM] * 6 + [HBM] * len(after),
        out_specs=VMEM,
        out_shape=jax.ShapeDtypeStruct(shape, BF16),
        compiler_params=pltpu.CompilerParams(vmem_limit_bytes=16 * 2**20),
    )(*second, *third, *after)


def inner_fwd_kernel(n, *refs):
    parts, (y, v, up2, down3) = refs[:n], refs[n : n + 4]
    full2, full3 = refs[n + 4 :]
    owned_c, nm, pair = full2.shape
    half, rows = pair // 2, y.shape[0]
    own2, own3 = nm // n, half // n

    @pl.when(pl.program_id(0) == 0)
    def _():
        for k in range(n):
            at2 = pl.multiple_of(owner(-k, n) * own2, own2)
            at3 = pl.multiple_of(owner(-k, n) * own3, own3)
            for c, piece, cols in each_piece2(owned_c, own2, pair):
                full2[c, pl.ds(at2, own2), cols] = parts[k][c, piece, :]
            for c, at, cols in each_piece3(owned_c, nm):
                full3[c, pl.ds(at3, own3), :] = parts[k][at, :, cols]
        for c in range(owned_c):
            hot = place_c(c, owned_c, rows, nm, BF16)
            up2[c * pair : (c + 1) * pair, :] = dot(full2[c], hot, 0, 1).astype(BF16)
            down3[:, c * half : (c + 1) * half] = dot(hot, full3[c], 1, 1).astype(BF16)

    block = y[...]
    total = None
    for c in range(owned_c):
        g = dot(up2[c * pair : (c + 1) * pair, :], block, 1, 0)
        gate, up = g[:half], g[half:]
        hidden = (gate * logistic(gate) * up).astype(BF16)
        term = dot(down3[:, c * half : (c + 1) * half], hidden, 1, 0)
        total = term if total is None else total + term
    v[...] = total.astype(BF16)


def inner_fwd(parts, y, n, owned_c, nm, half, tb):
    rows, tokens = y.shape
    pair = 2 * half
    fixed = lambda i: (0, 0)
    return pl.pallas_call(
        functools.partial(inner_fwd_kernel, n),
        grid=(tokens // tb,),
        in_specs=[VMEM] * n + [pl.BlockSpec((rows, tb), lambda i: (0, i))],
        out_specs=[
            pl.BlockSpec((rows, tb), lambda i: (0, i)),
            pl.BlockSpec((owned_c * pair, rows), fixed),
            pl.BlockSpec((rows, owned_c * half), fixed),
        ],
        out_shape=[
            pltpu.HBM((rows, tokens), BF16),
            pltpu.HBM((owned_c * pair, rows), BF16),
            pltpu.HBM((rows, owned_c * half), BF16),
        ],
        scratch_shapes=[pltpu.VMEM((owned_c, nm, pair), BF16), pltpu.VMEM((owned_c, half, nm), BF16)],
        compiler_params=params(32),
        cost_estimate=pl.CostEstimate(
            flops=6 * tokens * rows * owned_c * half, bytes_accessed=4 * tokens * rows, transcendentals=tokens * owned_c * half
        ),
    )(*parts, y)


def inner_bwd_kernel(n, owned_c, y, dv, up2, down3, dz, *refs):
    parts, (up3, down2, total2, total3) = refs[:n], refs[n:]
    rows = y.shape[0]
    nm, pair = rows // owned_c, up2.shape[0] // owned_c
    half = pair // 2
    own2, own3 = nm // n, half // n
    step = pl.program_id(0)

    @pl.when(step == 0)
    def _():
        total2[...] = jnp.zeros_like(total2)
        total3[...] = jnp.zeros_like(total3)
        up3[...] = down3[...].T
        down2[...] = up2[...].T

    block, back = y[...], dv[...]
    back_t = back.T
    total = None
    for c in range(owned_c):
        pairs, halves = slice(c * pair, (c + 1) * pair), slice(c * half, (c + 1) * half)
        g = dot(up2[pairs, :], block, 1, 0)
        gate, up = g[:half], g[half:]
        sigma = logistic(gate)
        silu = gate * sigma
        hidden = (silu * up).astype(BF16)
        total3[halves, :] += dot(hidden, back_t, 1, 0)
        dh = dot(up3[halves, :], back, 1, 0)
        d_gate = (dh * up * (sigma + silu * (1.0 - sigma))).astype(BF16)
        d_up = (dh * silu).astype(BF16)
        dg = jnp.concatenate([d_gate, d_up], axis=0)
        both = dot(block, dg, 1, 1)
        for piece in range(pair // LANES):
            total2[c * (pair // LANES) + piece] += both[:, piece * LANES : (piece + 1) * LANES]
        term = dot(down2[:, pairs], dg, 1, 0)
        total = term if total is None else total + term
    dz[...] = total.astype(BF16)

    @pl.when(step == pl.num_programs(0) - 1)
    def _():
        for k in range(n):
            at2 = owner(k, n) * (own2 * owned_c)
            for c, piece, cols in each_piece2(owned_c, own2, pair):
                held = total2.at[(c * pair + cols.start) // LANES]
                parts[k][c, piece, :] = held[pl.ds(at2 + c, own2, stride=owned_c), :]
        for c, at, cols in each_piece3(owned_c, nm):
            hot = place_c(c, owned_c, rows, nm, BF16)
            for k in range(n):
                at3 = pl.multiple_of(c * half + owner(k, n) * own3, own3)
                parts[k][at, :, cols] = picked(total3[pl.ds(at3, own3), :], hot, 1, 0)


def inner_bwd(y, dv, up2, down3, n, owned_c, tb):
    rows, tokens = y.shape
    pair, half, nm = up2.shape[0] // owned_c, down3.shape[1] // owned_c, rows // owned_c
    part = jax.ShapeDtypeStruct(pack_shape(owned_c, nm // n, pair, half // n, nm), F32)
    fixed = lambda i: (0, 0)
    fixed3 = lambda i: (0, 0, 0)
    return pl.pallas_call(
        functools.partial(inner_bwd_kernel, n, owned_c),
        grid=(tokens // tb,),
        in_specs=[
            pl.BlockSpec((rows, tb), lambda i: (0, i)),
            pl.BlockSpec((rows, tb), lambda i: (0, i)),
            pl.BlockSpec(up2.shape, fixed),
            pl.BlockSpec(down3.shape, fixed),
        ],
        out_specs=[pl.BlockSpec((rows, tb), lambda i: (0, i))] + [pl.BlockSpec(part.shape, fixed3)] * n,
        out_shape=[pltpu.HBM((rows, tokens), BF16)] + [pltpu.HBM(part.shape, part.dtype)] * n,
        scratch_shapes=[
            pltpu.VMEM((owned_c * half, rows), BF16),
            pltpu.VMEM((rows, owned_c * pair), BF16),
            pltpu.VMEM((owned_c * pair // LANES, rows, LANES), F32),
            pltpu.VMEM((owned_c * half, rows), F32),
        ],
        compiler_params=params(32),
        cost_estimate=pl.CostEstimate(
            flops=16 * tokens * rows * owned_c * half, bytes_accessed=6 * tokens * rows, transcendentals=tokens * owned_c * half
        ),
    )(y, dv, *(pltpu.with_memory_space_constraint(w, pltpu.HBM) for w in (up2, down3)))


def added(parts):
    total = parts[0]
    for part in parts[1:]:
        total = total + part
    return total


def finish_inner_kernel(n, *refs):
    parts, (rho2, noise2, rho3, noise3, mean2, grad2, mean3, grad3) = refs[:n], refs[n:]
    owned_c, own2, pair = rho2.shape
    for c, rows, cols in each_piece2(owned_c, own2, pair):
        total = added([part[c, rows, :] for part in parts])
        mean2[c, :, cols] = total
        grad2[c, :, cols] = total * noise2[c, :, cols] * logistic(rho2[c, :, cols])
    for c, at, cols in each_piece3(owned_c, rho3.shape[2]):
        total = added([part[at, :, cols] for part in parts])
        mean3[c] = total
        grad3[c] = total * noise3[c] * logistic(rho3[c])


def finish_inner(parts, rho2, noise2, rho3, noise3):
    n = len(parts)
    return pl.pallas_call(
        functools.partial(finish_inner_kernel, n),
        in_specs=[VMEM] * (n + 4),
        out_specs=[VMEM] * 4,
        out_shape=[jax.ShapeDtypeStruct(rho2.shape, F32)] * 2 + [jax.ShapeDtypeStruct(rho3.shape, F32)] * 2,
        compiler_params=pltpu.CompilerParams(vmem_limit_bytes=16 * 2**20),
    )(*parts, rho2, noise2, rho3, noise3)


def finish_kernel(n, *refs):
    parts, (rho, noise, mean_grad, rho_grad) = refs[:n], refs[n:]
    total = added([part[...] for part in parts])
    mean_grad[...] = total
    rho_grad[...] = total * noise[...] * logistic(rho[...])


def finish(parts, rho, noise):
    n = len(parts)
    return pl.pallas_call(
        functools.partial(finish_kernel, n),
        in_specs=[VMEM] * (n + 2),
        out_specs=[VMEM] * 2,
        out_shape=[jax.ShapeDtypeStruct(rho.shape, F32)] * 2,
        compiler_params=pltpu.CompilerParams(vmem_limit_bytes=16 * 2**20),
    )(*parts, rho, noise)


def shards(
    n,
    tokens,
    cotangent,
    first_mean,
    first_rho,
    first_noise,
    second_mean,
    second_rho,
    second_noise,
    third_mean,
    third_rho,
    third_noise,
    fourth_mean,
    fourth_rho,
    fourth_noise,
):
    owned_m, width = first_mean.shape[0], first_mean.shape[2]
    owned_c, nm = second_mean.shape[0], second_mean.shape[1] * n
    half = third_mean.shape[1] * n

    outer = jnp.concatenate(
        [sampled(first_mean, first_rho, first_noise), sampled(fourth_mean, fourth_rho, fourth_noise)], axis=0
    )
    outer_parts = gather_parts(outer, n)
    y_out, placed1 = outer_in(outer_parts, stash(tokens), n, owned_c, 1, 0)
    y = exchange(y_out)
    inner = sample_inner((second_mean, second_rho, second_noise), (third_mean, third_rho, third_noise), (placed1,))
    inner_parts = gather_parts(inner, n)
    back_out, placed4 = outer_in(outer_parts, cotangent, n, owned_c, 0, owned_m, inner_parts)
    back = exchange(back_out)
    v_out, up2, down3 = inner_fwd(inner_parts, y, n, owned_c, nm, half, 1024)
    v = exchange(v_out)
    dz_out, *shares = inner_bwd(y, back, up2, down3, n, owned_c, 1024)
    dz = exchange(dz_out)
    two_three = finish_inner(scatter_parts(shares, n), second_rho, second_noise, third_rho, third_noise)
    layer_out, *share4 = outer_out(v, cotangent, placed4, n, owned_m, owned_c, width, 2048)
    four = finish(scatter_parts(share4, n), fourth_rho, fourth_noise)
    share1 = outer_grad(dz, stash(tokens, (two_three[0], four[0])), n, owned_m, owned_c, width)
    one = finish(scatter_parts(share1, n), first_rho, first_noise)
    return (layer_out, *one, *two_three, *four)


def solution(mesh):
    block = P("block", "dp", None)
    rows = P("dp", "block")
    return jax.shard_map(
        functools.partial(shards, mesh.shape["dp"]),
        mesh=mesh,
        in_specs=(rows, rows) + (block,) * 12,
        out_specs=(rows,) + (block,) * 8,
        check_vma=False,
    )
```
